256 devices in a mesh: table: 64 (over y, x, z_lo, core), rep: 4 (over z_hi).
Axes of the slice: x: 4, y: 4, z: 8 (z_hi: 4, z_lo: 2; z = z_hi * 2 + z_lo), core: 2. Of those that a mesh axis runs over, the one named last changes fastest.
Arguments:
- pooled: bfloat16 [2048, 32768], P('rep', 'table'), may hold values from -6 to 6
- table_slot: int32 [256], replicated, may hold values from 0 to 255, each once
- cross_v: bfloat16 [32768, 256], P('table'), may hold values from -0.03125 to 0.03125
- cross_u: bfloat16 [256, 32768], P(None, 'table'), may hold values from -0.375 to 0.375
- cross_bias: float32 [32768], P('table'), may hold values from -3 to 3
- block_index1: int32 [256], replicated, may hold values from 0 to 255, each once
- weight1: bfloat16 [256, 128, 128], P('table'), may hold values from -0.1875 to 0.1875
- block_index2: int32 [128], replicated, may hold values from 0 to 31
- weight2: bfloat16 [128, 128, 128], P('table'), may hold values from -0.25 to 0.25
- top_vectors: float32 [3, 4096], replicated, may hold values from -0.6 to 0.6
- labels: int32 [4, 512], P('rep', 'table'), may hold values 0 or 1
- importance: int32 [4, 512], P('rep', 'table'), may hold values from 1 to 16
Outputs:
- d_pooled: bfloat16 [2048, 32768], P('rep', 'table')
- grad_v: float32 [32768, 256], P('table')
- grad_u: float32 [256, 32768], P(None, 'table')
- grad_bias: float32 [32768], P('table')
- grad_w1: float32 [256, 128, 128], P('table')
- grad_w2: float32 [128, 128, 128], P('table')
- grad_vectors: float32 [3, 4096], replicated
The draws below stay inside these ranges and needn't reach their ends.
All inputs are finite; a program needn't handle non-finite values. No bound on the sum of `labels` on one device may be relied on, other than what follows from the above.
Results may differ from the reference program's by a relative error of at most 0.024.
Values may be sent and summed in bfloat16 or wider, within the bound.
No kernel may reach another device: no remote copies, remote signals or barrier semaphores. Data moves between devices by JAX's collectives and lax.ppermute only.
A program may use at most 128 MiB of HBM per device.

```python
import jax
import jax.numpy as jnp
from jax import lax

E = 128
H = 4096
R = 256
K2 = 4
TABLES = 256
F = 32768
HB = 32
K1 = 8
NB1 = 256
NB2 = 128
GROUP = 512
BATCH = 2048
N_REP = 4


def with_ends(values, key, least, largest):
    longest = values.shape.index(max(values.shape))
    spots = []
    for shift in (0, 1):
        where = [jax.random.randint(jax.random.fold_in(key, axis), (), 0, length) for axis, length in enumerate(values.shape)]
        where[longest] = (where[longest] + shift) % values.shape[longest]
        spots.append(tuple(where))
    return values.at[spots[0]].set(least).at[spots[1]].set(largest)


def levels(key, dims, shards, smallest, high):
    loudness, own = 1.0, jax.random.fold_in(key, 6)
    for axis_at, blocks in shards:
        steps = jnp.exp(jax.random.uniform(jax.random.fold_in(own, axis_at), (blocks,), jnp.float32, smallest / len(shards), high / len(shards)))
        loudness = loudness * jnp.repeat(steps, dims[axis_at] // blocks).reshape([-1 if axis == axis_at else 1 for axis in range(len(dims))])
    return loudness


def centred(stream_key, extent, deviation, most, cuts=(), kind=jnp.bfloat16):
    result = jax.random.normal(stream_key, extent, jnp.float32) * deviation
    if len(cuts) > 0:
        result = levels(stream_key, extent, cuts, -0.22, 0.18) * result
    return jnp.clip(result, min=-most, max=most).astype(kind)


def setup_inputs(seed: int = 0) -> dict:
    arg_keys = jax.random.split(jax.random.key(seed), 13)
    return {
        "pooled": centred(arg_keys[0], (BATCH, F), 1.0, 6.0, ((0, 4), (1, 64))),
        "table_slot": jax.random.permutation(arg_keys[1], TABLES).astype(jnp.int32),
        "cross_v": centred(arg_keys[2], (F, R), F ** -0.5, 0.03125, ((0, 64),)),
        "cross_u": centred(arg_keys[3], (R, F), R ** -0.5, 0.375, ((1, 64),)),
        "cross_bias": centred(arg_keys[4], (F,), 0.5, 3.0, ((0, 64),), jnp.float32),
        "block_index1": jax.random.permutation(arg_keys[5], TABLES).astype(jnp.int32),
        "weight1": centred(arg_keys[6], (NB1, E, E), (K1 * E) ** -0.5, 0.1875, ((0, 64),)),
        "block_index2": with_ends(jax.random.randint(arg_keys[7], (NB2,), 0, HB), jax.random.fold_in(arg_keys[7], 1), 0, HB - 1).astype(jnp.int32),
        "weight2": centred(arg_keys[8], (NB2, E, E), (K2 * E) ** -0.5, 0.25, ((0, 64),)),
        "top_vectors": centred(arg_keys[9], (3, H), 0.1, 0.6, (), jnp.float32),
        "labels": with_ends((jax.random.randint(arg_keys[10], (N_REP, GROUP), 0, 2) < 1).astype(jnp.int32), jax.random.fold_in(arg_keys[10], 1), 0, 1),
        "importance": with_ends(jax.random.randint(arg_keys[11], (N_REP, GROUP), 1, 17), jax.random.fold_in(arg_keys[11], 1), 1, 16).astype(jnp.int32),
    }


def silu_slope(value):
    squash = jax.nn.sigmoid(value)
    return squash * (1.0 + value * (1.0 - squash))


def block_forward(blocks, columns, weight, per_column, offset):
    batch_rows = blocks.shape[0]
    picked = blocks[:, columns]
    block_terms = jnp.einsum("bnc,ncd->bnd", picked.astype(jnp.float32), weight.astype(jnp.float32))
    summed = block_terms.reshape(batch_rows, -1, per_column, E).sum(axis=2)
    return summed + offset.reshape(-1, E), picked


def reference(pooled, table_slot, cross_v, cross_u, cross_bias, block_index1, weight1, block_index2, weight2, top_vectors, labels, importance):
    batch_rows = pooled.shape[0]
    slot_of = jnp.argsort(table_slot.astype(jnp.int32)).astype(jnp.int32)
    columns_one = jnp.take(slot_of, block_index1.astype(jnp.int32)).astype(jnp.int32)
    crossed = jnp.dot(pooled, cross_v, preferred_element_type=jnp.float32).astype(jnp.bfloat16)
    factor = jnp.dot(crossed, cross_u, preferred_element_type=jnp.float32) + cross_bias + 1.0
    lifted = (pooled.astype(jnp.float32) * factor).astype(jnp.bfloat16)
    lifted_blocks = lifted.reshape(batch_rows, TABLES, E)
    preact_one, picked_one = block_forward(lifted_blocks, columns_one, weight1, K1, top_vectors[0])
    hidden_one = jax.nn.silu(preact_one).astype(jnp.bfloat16)
    preact_two, picked_two = block_forward(hidden_one, block_index2.astype(jnp.int32), weight2, K2, top_vectors[1])
    hidden_two = jax.nn.silu(preact_two).astype(jnp.bfloat16)
    last_weight = top_vectors[2].reshape(-1, E)
    logit = jnp.sum(hidden_two.astype(jnp.float32) * last_weight, axis=(1, 2))
    sample_weight = importance.reshape(-1).astype(jnp.float32) / 8.0
    targets = labels.reshape(-1).astype(jnp.float32)
    grad_logit = sample_weight * (jax.nn.sigmoid(logit) - targets)
    grad_two = (grad_logit[:, None, None] * last_weight * silu_slope(preact_two)).astype(jnp.bfloat16)
    spread_two = jnp.repeat(grad_two, K2, axis=1)
    grad_w2 = jnp.einsum("bnc,bnd->ncd", picked_two.astype(jnp.float32), spread_two.astype(jnp.float32))
    back_two = jnp.einsum("bnd,ncd->bnc", spread_two.astype(jnp.float32), weight2.astype(jnp.float32))
    onehot_two = (block_index2.astype(jnp.int32)[:, None] == jnp.arange(HB, dtype=jnp.int32)[None, :]).astype(jnp.float32)
    into_one = jnp.einsum("bnc,nj->bjc", back_two, onehot_two, precision=lax.Precision.HIGHEST)
    grad_one = (into_one * silu_slope(preact_one)).astype(jnp.bfloat16)
    spread_one = jnp.repeat(grad_one, K1, axis=1)
    grad_w1 = jnp.einsum("bnc,bnd->ncd", picked_one.astype(jnp.float32), spread_one.astype(jnp.float32))
    back_one = jnp.einsum("bnd,ncd->bnc", spread_one.astype(jnp.float32), weight1.astype(jnp.float32))
    onehot_one = (columns_one[:, None] == jnp.arange(TABLES, dtype=jnp.int32)[None, :]).astype(jnp.float32)
    into_lifted = jnp.einsum("bnc,ns->bsc", back_one, onehot_one, precision=lax.Precision.HIGHEST)
    grad_lifted = into_lifted.reshape(batch_rows, -1).astype(jnp.bfloat16)
    cross_grad = grad_lifted.astype(jnp.float32) * pooled.astype(jnp.float32)
    cross_half = cross_grad.astype(jnp.bfloat16)
    direct = grad_lifted.astype(jnp.float32) * factor
    grad_crossed = jnp.dot(cross_half, cross_u.T, preferred_element_type=jnp.float32).astype(jnp.bfloat16)
    grad_u = jnp.dot(crossed.T, cross_half, preferred_element_type=jnp.float32)
    grad_bias = jnp.sum(cross_grad, axis=0)
    grad_v = jnp.dot(pooled.T, grad_crossed, preferred_element_type=jnp.float32)
    d_pooled = (direct + jnp.dot(grad_crossed, cross_v.T, preferred_element_type=jnp.float32)).astype(jnp.bfloat16)
    grad_vectors = jnp.stack([
        jnp.sum(grad_one.astype(jnp.float32), axis=0).reshape(-1),
        jnp.sum(grad_two.astype(jnp.float32), axis=0).reshape(-1),
        jnp.sum(hidden_two.astype(jnp.float32) * grad_logit[:, None, None], axis=0).reshape(-1),
    ])
    return d_pooled, grad_v, grad_u, grad_bias, grad_w1, grad_w2, grad_vectors
```

```python
import jax
import jax.numpy as jnp
from jax import lax
from jax.sharding import PartitionSpec as P

E = 128
K1 = 8
K2 = 4
HB = 32
NT = 64
N_REP = 4
BF = jnp.bfloat16
F32 = jnp.float32


def silu_slope(value):
    squash = jax.nn.sigmoid(value)
    return squash * (1.0 + value * (1.0 - squash))


def exchange(parts):
    return lax.all_to_all(parts, "table", split_axis=0, concat_axis=0, tiled=True)


def from_rep(value, shift):
    return lax.ppermute(value, "rep", [(i, (i + shift) % N_REP) for i in range(N_REP)])


def rep_sum_scatter(quarters):
    mine = lax.axis_index("rep")
    total = lax.dynamic_index_in_dim(quarters, mine, 0, keepdims=False).astype(F32)
    for shift in (1, 2, 3):
        sent = lax.dynamic_index_in_dim(quarters, (mine + shift) % N_REP, 0, keepdims=False)
        total = total + from_rep(sent, shift).astype(F32)
    return total.astype(BF)


def rep_gather(quarter):
    mine = lax.axis_index("rep")
    whole = jnp.zeros((N_REP,) + quarter.shape, BF)
    whole = lax.dynamic_update_index_in_dim(whole, quarter, mine, 0)
    for shift in (1, 2, 3):
        whole = lax.dynamic_update_index_in_dim(
            whole, from_rep(quarter, shift), (mine - shift) % N_REP, 0
        )
    return whole


def split_pieces(blocks):
    return blocks.reshape(4, NT, 2, E).transpose(1, 0, 2, 3).reshape(NT, 8, E)


def join_pieces(pieces):
    return pieces.reshape(NT, 4, 2, E).transpose(1, 0, 2, 3).reshape(4, E, E)


def reorder(pieces, select):
    rows = pieces.reshape(NT * 4, 2 * E)
    moved = jnp.dot(select, rows, preferred_element_type=F32).astype(BF)
    return moved.reshape(NT, 8, E)


def body(
    pooled,
    table_slot,
    cross_v,
    cross_u,
    cross_bias,
    block_index1,
    weight1,
    block_index2,
    weight2,
    top_vectors,
    labels,
    importance,
):
    tables = table_slot.shape[0]
    contract_last = (((1,), (1,)), ((), ()))
    contract_first = (((0,), (0,)), ((), ()))
    full_two = lax.all_gather(weight2, "table", axis=0, tiled=True)

    reads = block_index1[:, None] == table_slot[None, :]
    reads_half = reads.astype(BF)
    hidden_of_slot = jnp.sum(
        jnp.where(reads, jnp.arange(tables, dtype=jnp.int32)[:, None] // K1, 0), axis=0
    )
    adds = (jnp.arange(HB, dtype=jnp.int32)[:, None] == hidden_of_slot[None, :]).astype(BF)

    partial = jnp.dot(pooled, cross_v, preferred_element_type=F32).astype(BF)
    got = exchange(
        jnp.concatenate([partial.reshape(NT, 8, 256), split_pieces(weight1)], axis=2)
    )
    crossed_own = jnp.sum(got[:, :, :256].astype(F32), axis=0).astype(BF)
    by_slot = reorder(got[:, :, 256:], reads_half.T)
    got = exchange(
        jnp.concatenate([jnp.broadcast_to(crossed_own[None], (NT, 8, 256)), by_slot], axis=2)
    )
    crossed = got[:, :, :256].reshape(512, 256)
    weight_slot = join_pieces(got[:, :, 256:])

    factor = jnp.dot(crossed, cross_u, preferred_element_type=F32) + cross_bias + 1.0
    lifted = (pooled.astype(F32) * factor).astype(BF)
    lifted_blocks = lifted.reshape(512, 4, E)
    terms = jnp.einsum("bqc,qcd->bqd", lifted_blocks, weight_slot, preferred_element_type=F32)
    got = exchange(terms.astype(BF).reshape(NT, 8, 512))
    terms_own = got.reshape(NT, 8, 4, E).transpose(0, 2, 1, 3).reshape(tables, 8 * E)
    preact_one = jnp.dot(adds, terms_own, preferred_element_type=F32).reshape(HB, 8, E)
    preact_one = preact_one.transpose(1, 0, 2) + top_vectors[0].reshape(-1, E)
    hidden_one = jax.nn.silu(preact_one).astype(BF)

    picked_two = hidden_one[:, block_index2]
    terms_two = jnp.einsum("bnc,ncd->bnd", picked_two, full_two, preferred_element_type=F32)
    preact_two = terms_two.reshape(8, HB, K2, E).sum(axis=2) + top_vectors[1].reshape(-1, E)
    hidden_two = jax.nn.silu(preact_two).astype(BF)
    last_weight = top_vectors[2].reshape(-1, E)
    logit = jnp.sum(hidden_two.astype(F32) * last_weight, axis=(1, 2))
    sample_weight = importance.reshape(-1).astype(F32) / 8.0
    targets = labels.reshape(-1).astype(F32)
    grad_logit = sample_weight * (jax.nn.sigmoid(logit) - targets)
    grad_two = (grad_logit[:, None, None] * last_weight * silu_slope(preact_two)).astype(BF)
    last_terms = (hidden_two.astype(F32) * grad_logit[:, None, None]).astype(BF)
    spread_two = jnp.repeat(grad_two, K2, axis=1)
    back_two = jnp.einsum("bnd,ncd->bnc", spread_two, full_two, preferred_element_type=F32)
    onehot_two = (block_index2[:, None] == jnp.arange(HB, dtype=jnp.int32)[None, :]).astype(F32)
    into_one = jnp.einsum("bnc,nj->bjc", back_two, onehot_two, precision=lax.Precision.HIGHEST)
    grad_one = (into_one * silu_slope(preact_one)).astype(BF)

    spread_one = grad_one[:, hidden_of_slot].reshape(8, NT, 4 * E)
    picked_pair = picked_two.reshape(8, NT, 2 * E)
    both = jnp.repeat(grad_two, 2, axis=1)
    third = jnp.stack([grad_one, last_terms], axis=2).reshape(8, NT, E)
    sent = jnp.concatenate([spread_one, picked_pair, both, third], axis=2).transpose(1, 0, 2)
    got = exchange(sent).reshape(512, 8 * E)
    grad_rows = got[:, : 4 * E]
    hidden_rows = got[:, 4 * E : 6 * E]
    two_rows = got[:, 6 * E : 7 * E]
    third_rows = got[:, 7 * E :]

    grad_rows_blocks = grad_rows.reshape(512, 4, E)
    back_one = jnp.einsum(
        "bqd,qcd->bqc", grad_rows_blocks, weight_slot, preferred_element_type=F32
    )
    grad_lifted = back_one.astype(BF).reshape(512, 512)
    local_one = jnp.einsum(
        "bqc,bqd->qcd", lifted_blocks, grad_rows_blocks, preferred_element_type=F32
    )
    local_two = lax.dot_general(
        hidden_rows, two_rows, contract_first, preferred_element_type=F32
    )
    vector_rows = jnp.stack(
        [jnp.sum(two_rows.astype(F32), axis=0), jnp.sum(third_rows.astype(F32), axis=0)]
    )
    vector_sum = (vector_rows + from_rep(vector_rows, 2)) + (
        from_rep(vector_rows, 1) + from_rep(vector_rows, 3)
    )

    cross_grad = grad_lifted.astype(F32) * pooled.astype(F32)
    cross_half = cross_grad.astype(BF)
    direct = grad_lifted.astype(F32) * factor
    partial_back = lax.dot_general(
        cross_half, cross_u, contract_last, preferred_element_type=F32
    ).astype(BF)
    got = exchange(
        jnp.concatenate(
            [partial_back.reshape(NT, 8, 256), split_pieces(local_one.astype(BF))], axis=2
        )
    )
    back_own = jnp.sum(got[:, :, :256].astype(F32), axis=0).astype(BF)
    by_block = reorder(got[:, :, 256:], reads_half)
    shared = jnp.concatenate(
        [back_own, jnp.pad(vector_sum.astype(BF), ((0, 6), (0, 0)))], axis=1
    )

    local_u = lax.dot_general(crossed, cross_half, contract_first, preferred_element_type=F32)
    local_bias = jnp.sum(cross_grad, axis=0)
    early = jnp.concatenate(
        [
            local_u.astype(BF).reshape(N_REP, 64, 512),
            local_two.astype(BF).reshape(N_REP, 16, 512),
            jnp.pad(local_bias.astype(BF).reshape(N_REP, 1, 128), ((0, 0), (0, 7), (0, 384))),
        ],
        axis=1,
    )
    early_quarter = rep_sum_scatter(early)

    got = exchange(
        jnp.concatenate([jnp.broadcast_to(shared[None], (NT, 8, 384)), by_block], axis=2)
    )
    grad_crossed = got[:, :, :256].reshape(512, 256)
    vectors = got[:, :2, 256:384].astype(F32)
    summed_one = join_pieces(got[:, :, 384:])
    early_whole = rep_gather(early_quarter)

    local_v = lax.dot_general(pooled, grad_crossed, contract_first, preferred_element_type=F32)
    late = jnp.concatenate(
        [
            local_v.astype(BF).reshape(N_REP, 128, 256),
            summed_one.reshape(N_REP, 64, 256),
        ],
        axis=1,
    )
    late_whole = rep_gather(rep_sum_scatter(late))
    d_pooled = (
        direct + lax.dot_general(grad_crossed, cross_v, contract_last, preferred_element_type=F32)
    ).astype(BF)

    grad_u = early_whole[:, :64].reshape(256, 512).astype(F32)
    grad_w2 = early_whole[:, 64:80].reshape(2, E, E).astype(F32)
    grad_bias = early_whole[:, 80, :128].reshape(512).astype(F32)
    grad_v = late_whole[:, :128].reshape(512, 256).astype(F32)
    grad_w1 = late_whole[:, 128:].reshape(4, E, E).astype(F32)
    pairs = vectors.reshape(HB, 2, 2, E)
    grad_vectors = jnp.stack(
        [pairs[:, 0, 1].reshape(-1), pairs[:, 0, 0].reshape(-1), pairs[:, 1, 1].reshape(-1)]
    )
    return (d_pooled, grad_v, grad_u, grad_bias, grad_w1, grad_w2, grad_vectors)


def solution(mesh):
    placed = (
        P("rep", "table"),
        P(),
        P("table", None),
        P(None, "table"),
        P("table"),
        P(),
        P("table", None, None),
        P(),
        P("table", None, None),
        P(),
        P("rep", "table"),
        P("rep", "table"),
    )
    return jax.shard_map(
        body,
        mesh=mesh,
        in_specs=placed,
        out_specs=(
            P("rep", "table"),
            P("table", None),
            P(None, "table"),
            P("table"),
            P("table", None, None),
            P("table", None, None),
            P(),
        ),
        check_vma=False,
    )
```

```python
import jax
import jax.numpy as jnp
from jax import lax
from jax.experimental import pallas as pl
from jax.experimental.pallas import tpu as pltpu
from jax.sharding import PartitionSpec as P

E = 128
K1 = 8
K2 = 4
HB = 32
NT = 64
N_REP = 4
BF = jnp.bfloat16
F32 = jnp.float32


def silu_slope(value):
    squash = jax.nn.sigmoid(value)
    return squash * (1.0 + value * (1.0 - squash))


def exchange(parts):
    return lax.all_to_all(parts, "table", split_axis=0, concat_axis=0, tiled=True)


def from_sibling(value):
    return lax.ppermute(value, "table", [(i, i ^ 1) for i in range(NT)])


def one_hot_rows(shape, source):
    row = lax.broadcasted_iota(jnp.int32, shape, 0)
    col = lax.broadcasted_iota(jnp.int32, shape, 1)
    return (source(row) == col).astype(F32).astype(BF)


def move_rows(order, rows):
    return jnp.dot(order, rows, preferred_element_type=F32).astype(BF)


def to_pieces(row):
    return ((row >> 1) & 3) * E + (row >> 3) * 2 + (row & 1)


def to_blocks(row):
    return ((row & 127) >> 1) * 8 + (row >> 7) * 2 + (row & 1)


def lift_kernel(got_ref, pooled_ref, u_ref, bias_ref, lifted_ref, factor_ref, terms_ref, weight_ref):
    weight = move_rows(one_hot_rows((512, 512), to_blocks), got_ref[:, 256:384])
    weight_ref[...] = weight
    factor = jnp.dot(got_ref[:, :256], u_ref[...], preferred_element_type=F32) + bias_ref[...] + 1.0
    factor_ref[...] = factor
    lifted = (pooled_ref[...].astype(F32) * factor).astype(BF)
    lifted_ref[...] = lifted
    for q in range(4):
        cols = slice(q * E, (q + 1) * E)
        terms_ref[:, cols] = jnp.dot(
            lifted[:, cols], weight[cols], preferred_element_type=F32
        ).astype(BF)


def whole(shape):
    return pl.BlockSpec(shape, lambda i: (0,) * len(shape))


def call(kernel, shapes, *values):
    return pl.pallas_call(
        kernel,
        grid=(1,),
        out_shape=shapes,
        in_specs=[whole(value.shape) for value in values],
        out_specs=[whole(shape.shape) for shape in shapes],
        compiler_params=pltpu.CompilerParams(vmem_limit_bytes=48 * 1024 * 1024),
    )(*values)


def lift(got, pooled, cross_u, bias):
    shapes = [((512, 512), BF), ((512, 512), F32), ((512, 512), BF), ((512, E), BF)]
    return call(
        lift_kernel,
        [jax.ShapeDtypeStruct(*shape) for shape in shapes],
        got,
        pooled,
        cross_u,
        bias,
    )


def first_kernel(got_ref, adds_ref, bias_ref, preact_ref, hidden_ref):
    total = jnp.broadcast_to(bias_ref[...][:, None, :], (HB, 8, E)).reshape(HB * 8, E)
    for q in range(4):
        total = total + jnp.dot(
            adds_ref[q], got_ref[:, q * E : (q + 1) * E], preferred_element_type=F32
        )
    preact_ref[...] = total
    hidden_ref[...] = (total * jax.nn.sigmoid(total)).astype(BF)


def hidden_first(got, adds, bias):
    return call(
        first_kernel,
        [jax.ShapeDtypeStruct((HB * 8, E), F32), jax.ShapeDtypeStruct((HB * 8, E), BF)],
        got,
        adds,
        bias,
    )


def start_kernel(pooled_ref, v_ref, weight_ref, pair_ref, out_ref):
    out_ref[:, :256] = jnp.dot(
        pooled_ref[...], v_ref[...], preferred_element_type=F32
    ).astype(BF)
    out_ref[:, 256:384] = move_rows(one_hot_rows((512, 512), to_pieces), weight_ref[...])
    pair = pair_ref[...]
    for i in range(32):
        out_ref[16 * i : 16 * i + 16, 384:] = pair


def regroup_kernel(got_ref, index_ref, extra_ref, out_ref):
    own = jnp.sum(got_ref[:, :256].astype(F32).reshape(NT, 8, 256), axis=0)
    own = jnp.concatenate([own, extra_ref[...]], axis=1) if extra_ref is not None else own
    width = own.shape[1]
    out_ref[:, :width] = (
        jnp.broadcast_to(own[None], (NT, 8, width)).reshape(512, width).astype(BF)
    )
    row = lax.broadcasted_iota(jnp.int32, (512, 512), 0)
    col = lax.broadcasted_iota(jnp.int32, (512, 512), 1)
    order = (index_ref[...] == (col >> 1)) & ((row & 1) == (col & 1))
    out_ref[:, width:] = move_rows(order.astype(F32).astype(BF), got_ref[:, 256:384])


def regroup(got, index, extra=None):
    kernel = regroup_kernel if extra is not None else (
        lambda got_ref, index_ref, out_ref: regroup_kernel(got_ref, index_ref, None, out_ref)
    )
    values = (got, index) if extra is None else (got, index, extra)
    width = 384 if extra is None else 512
    return pl.pallas_call(
        kernel,
        grid=(1,),
        out_shape=jax.ShapeDtypeStruct((512, width), BF),
        in_specs=[pl.BlockSpec((512, 384), lambda i: (0, 0))]
        + [pl.BlockSpec(value.shape, lambda i: (0, 0)) for value in values[1:]],
        out_specs=pl.BlockSpec((512, width), lambda i: (0, 0)),
        compiler_params=pltpu.CompilerParams(vmem_limit_bytes=48 * 1024 * 1024),
    )(*values)


def contract(left, right, at):
    return lax.dot_general(left, right, (((at,), (at,)), ((), ())), preferred_element_type=F32)


def owner_kernel(
    got_ref,
    weight_ref,
    lifted_ref,
    pooled_ref,
    factor_ref,
    crossed_ref,
    u_ref,
    sent_ref,
    direct_ref,
    up_ref,
    two_ref,
    vector_ref,
    bias_ref,
):
    crossed = crossed_ref[:, :256]
    back = jnp.zeros((512, 256), F32)
    blocks = []
    bias_ref[...] = jnp.zeros_like(bias_ref)
    for q in range(4):
        cols = slice(q * E, (q + 1) * E)
        rows = got_ref[:, cols]
        lifted_grad = contract(rows, weight_ref[cols, :], 1).astype(BF).astype(F32)
        cross_grad = lifted_grad * pooled_ref[:, cols].astype(F32)
        cross_half = cross_grad.astype(BF)
        direct_ref[:, cols] = lifted_grad * factor_ref[:, cols]
        back = back + contract(cross_half, u_ref[:, cols], 1)
        blocks.append(contract(lifted_ref[:, cols], rows, 0).astype(BF))
        up_ref[:, cols] = contract(crossed, cross_half, 0).astype(BF)
        bias_ref[q : q + 1, :] = jnp.sum(cross_grad, axis=0, keepdims=True)
    sent_ref[:, :256] = back.astype(BF)
    sent_ref[:, 256:] = move_rows(
        one_hot_rows((512, 512), to_pieces), jnp.concatenate(blocks, axis=0)
    )
    two_rows = got_ref[:, 6 * E : 7 * E]
    two_ref[...] = contract(got_ref[:, 4 * E : 6 * E], two_rows, 0).astype(BF)
    vector_ref[...] = jnp.concatenate(
        [
            jnp.sum(two_rows.astype(F32), axis=0, keepdims=True),
            jnp.sum(got_ref[:, 7 * E :].astype(F32), axis=0, keepdims=True),
            jnp.zeros((6, E), F32),
        ],
        axis=0,
    )


QUARTER = 368


def late_kernel(got_ref, pooled_ref, up_ref, two_ref, bias_ref, late_ref):
    local_v = contract(pooled_ref[...], got_ref[:, :256], 0).astype(BF)
    blocks = move_rows(one_hot_rows((512, 512), to_blocks), got_ref[:, 384:])

    def vector_source(row):
        place = (row >> 5) * 24 + (row & 31)
        which = place >> 5
        hidden = place & 31
        return 16 * hidden + jnp.where(which == 2, 8, 0) + jnp.where(which == 1, 0, 1)

    order = one_hot_rows((E, 512), vector_source)
    vectors = jnp.dot(order, got_ref[:, 256:384], preferred_element_type=F32)
    in_quarter = lax.broadcasted_iota(jnp.int32, (32, E), 0)
    for k in range(4):
        base = QUARTER * k
        late_ref[base : base + 128, :] = local_v[128 * k : 128 * k + 128]
        small = vectors[32 * k : 32 * k + 32]
        small = jnp.where(in_quarter == 24, bias_ref[k : k + 1, :], small).astype(BF)
        for side in range(2):
            cols = slice(side * E, (side + 1) * E)
            at = 128 * k + 64 * side
            late_ref[base + 128 : base + 192, cols] = blocks[at : at + 64]
            late_ref[base + 192 : base + 208, cols] = small[16 * side : 16 * side + 16]
            at = base + 208 + 64 * side
            late_ref[at : at + 64, :] = up_ref[64 * k : 64 * k + 64, 256 * side : 256 * side + 256]
            at = 64 * k + 32 * side
            late_ref[base + 336 : base + 368, cols] = two_ref[at : at + 32, :]


def add_kernel(got_ref, out_ref):
    total = got_ref[:QUARTER, :].astype(F32)
    for k in range(1, 4):
        total = total + got_ref[QUARTER * k : QUARTER * (k + 1), :].astype(F32)
    for k in range(4):
        out_ref[QUARTER * k : QUARTER * (k + 1), :] = total.astype(BF)


def last_kernel(got_ref, v_ref, one_ref, small_ref, up_ref, two_ref):
    for k in range(4):
        base = QUARTER * k
        v_ref[128 * k : 128 * k + 128, :] = got_ref[base : base + 128, :].astype(F32)
        for side in range(2):
            cols = slice(side * E, (side + 1) * E)
            at = 128 * k + 64 * side
            one_ref[at : at + 64, :] = got_ref[base + 128 : base + 192, cols].astype(F32)
            at = 32 * k + 16 * side
            small_ref[at : at + 16, :] = got_ref[base + 192 : base + 208, cols].astype(F32)
            at = base + 208 + 64 * side
            up_ref[64 * k : 64 * k + 64, 256 * side : 256 * side + 256] = got_ref[
                at : at + 64, :
            ].astype(F32)
            at = 64 * k + 32 * side
            two_ref[at : at + 32, :] = got_ref[base + 336 : base + 368, cols].astype(F32)


def body(
    pooled,
    table_slot,
    cross_v,
    cross_u,
    cross_bias,
    block_index1,
    weight1,
    block_index2,
    weight2,
    top_vectors,
    labels,
    importance,
):
    tables = table_slot.shape[0]
    contract_last = (((1,), (1,)), ((), ()))
    core = lax.axis_index("table") % 2
    half_index = lax.dynamic_index_in_dim(block_index2.reshape(HB, 2, 2), core, 2, keepdims=False)
    half_index = half_index.reshape(-1)

    reads = block_index1[:, None] == table_slot[None, :]
    numbers = jnp.arange(tables, dtype=jnp.int32)
    block_of_slot = jnp.sum(jnp.where(reads, numbers[:, None], 0), axis=0)
    slot_of_block = jnp.sum(jnp.where(reads, numbers[None, :], 0), axis=1)
    block_of_slot = jnp.repeat(block_of_slot, 2)[:, None]
    slot_of_block = jnp.repeat(slot_of_block, 2)[:, None]
    hidden_of_slot = jnp.sum(
        jnp.where(reads, jnp.arange(tables, dtype=jnp.int32)[:, None] // K1, 0), axis=0
    )
    out_row = lax.broadcasted_iota(jnp.int32, (4, HB * 8, NT * 8), 1)
    in_row = lax.broadcasted_iota(jnp.int32, (4, HB * 8, NT * 8), 2)
    wanted = jnp.repeat(hidden_of_slot.reshape(NT, 4).T, 8, axis=1)[:, None, :]
    adds = ((wanted == out_row // 8) & (out_row % 8 == in_row % 8)).astype(BF)

    pair_two = weight2.reshape(2, 16, 8, E).transpose(0, 2, 1, 3).reshape(16, 16 * E)
    (sent,) = call(
        start_kernel,
        [jax.ShapeDtypeStruct((512, 2432), BF)],
        pooled,
        cross_v,
        weight1.reshape(512, E),
        pair_two,
    )
    got = exchange(sent.reshape(NT, 8, 2432))
    half_two = got[:, :, 384:].reshape(NT, 8, 16, E).transpose(0, 2, 1, 3).reshape(NT, E, E)
    sent = regroup(got.reshape(512, 2432), block_of_slot)
    arrived = exchange(sent.reshape(NT, 8, 384)).reshape(512, 384)
    lifted, factor, terms, weight_slot = lift(
        arrived, pooled, cross_u, cross_bias.reshape(1, 512)
    )
    got = exchange(terms.reshape(NT, 8, 512))
    preact_one, hidden_one = hidden_first(
        got.reshape(512, 512), adds, top_vectors[0].reshape(HB, E)
    )
    preact_one = preact_one.reshape(HB, 8, E).transpose(1, 0, 2)
    hidden_one = hidden_one.reshape(HB, 8, E).transpose(1, 0, 2)
    hidden_both = jnp.concatenate([hidden_one, from_sibling(hidden_one)], axis=0)
    picked_both = hidden_both[:, half_index]
    terms_two = jnp.einsum("bnc,ncd->bnd", picked_both, half_two, preferred_element_type=F32)
    half_sum = terms_two.reshape(16, HB, 2, E).sum(axis=2)
    preact_two = half_sum[:8] + from_sibling(half_sum[8:]) + top_vectors[1].reshape(-1, E)
    hidden_two = jax.nn.silu(preact_two).astype(BF)
    last_weight = top_vectors[2].reshape(-1, E)
    logit = jnp.sum(hidden_two.astype(F32) * last_weight, axis=(1, 2))
    sample_weight = importance.reshape(-1).astype(F32) / 8.0
    targets = labels.reshape(-1).astype(F32)
    grad_logit = sample_weight * (jax.nn.sigmoid(logit) - targets)
    grad_two = (grad_logit[:, None, None] * last_weight * silu_slope(preact_two)).astype(BF)
    last_terms = (hidden_two.astype(F32) * grad_logit[:, None, None]).astype(BF)
    grad_both = jnp.concatenate([grad_two, from_sibling(grad_two)], axis=0)
    spread_two = jnp.repeat(grad_both, 2, axis=1)
    back_two = jnp.einsum("bnd,ncd->bnc", spread_two, half_two, preferred_element_type=F32)
    onehot_two = (half_index[:, None] == jnp.arange(HB, dtype=jnp.int32)[None, :]).astype(F32)
    half_into = jnp.einsum("bnc,nj->bjc", back_two, onehot_two, precision=lax.Precision.HIGHEST)
    into_one = half_into[:8] + from_sibling(half_into[8:])
    grad_one = (into_one * silu_slope(preact_one)).astype(BF)

    spread_one = grad_one[:, hidden_of_slot].reshape(8, NT, 4 * E)
    picked_pair = hidden_one[:, block_index2].reshape(8, NT, 2 * E)
    both = jnp.repeat(grad_two, 2, axis=1)
    third = jnp.stack([grad_one, last_terms], axis=2).reshape(8, NT, E)
    sent = jnp.concatenate([spread_one, picked_pair, both, third], axis=2).transpose(1, 0, 2)
    got = exchange(sent).reshape(512, 8 * E)
    sent, direct, local_u, local_two, vector_rows, local_bias = call(
        owner_kernel,
        [
            jax.ShapeDtypeStruct((512, 384), BF),
            jax.ShapeDtypeStruct((512, 512), F32),
            jax.ShapeDtypeStruct((256, 512), BF),
            jax.ShapeDtypeStruct((256, E), BF),
            jax.ShapeDtypeStruct((8, E), F32),
            jax.ShapeDtypeStruct((8, E), F32),
        ],
        got,
        weight_slot,
        lifted,
        pooled,
        factor,
        arrived,
        cross_u,
    )
    got = exchange(sent.reshape(NT, 8, 384))
    sent = regroup(got.reshape(512, 384), slot_of_block, vector_rows)
    got = exchange(sent.reshape(NT, 8, 512)).reshape(512, 512)
    grad_crossed = got[:, :256]
    parts = [jax.ShapeDtypeStruct((4 * QUARTER, 256), BF)]
    (late,) = call(late_kernel, parts, got, pooled, local_u, local_two, local_bias)
    late = lax.all_to_all(late, "rep", split_axis=0, concat_axis=0, tiled=True)
    (late,) = call(add_kernel, parts, late)
    late = lax.all_to_all(late, "rep", split_axis=0, concat_axis=0, tiled=True)
    shapes = [(512, 256), (512, E), (E, E), (256, 512), (256, E)]
    grad_v, grad_w1, small, grad_u, grad_w2 = call(
        last_kernel, [jax.ShapeDtypeStruct(shape, F32) for shape in shapes], late
    )
    d_pooled = (
        direct + lax.dot_general(grad_crossed, cross_v, contract_last, preferred_element_type=F32)
    ).astype(BF)

    grad_w1 = grad_w1.reshape(4, E, E)
    grad_w2 = grad_w2.reshape(2, E, E)
    small = small.reshape(4, 32, E)
    grad_bias = small[:, 24].reshape(512)
    grad_vectors = small[:, :24].reshape(3, HB * E)
    return (d_pooled, grad_v, grad_u, grad_bias, grad_w1, grad_w2, grad_vectors)


def solution(mesh):
    placed = (
        P("rep", "table"),
        P(),
        P("table", None),
        P(None, "table"),
        P("table"),
        P(),
        P("table", None, None),
        P(),
        P("table", None, None),
        P(),
        P("rep", "table"),
        P("rep", "table"),
    )
    return jax.shard_map(
        body,
        mesh=mesh,
        in_specs=placed,
        out_specs=(
            P("rep", "table"),
            P("table", None),
            P(None, "table"),
            P("table"),
            P("table", None, None),
            P("table", None, None),
            P(),
        ),
        check_vma=False,
    )
```

```python
import jax
import jax.numpy as jnp
from jax import lax
from jax.experimental import pallas as pl
from jax.experimental.pallas import tpu as pltpu
from jax.sharding import PartitionSpec as P

E = 128
K1 = 8
K2 = 4
HB = 32
NT = 64
N_REP = 4
BF = jnp.bfloat16
F32 = jnp.float32


def silu_slope(value):
    squash = jax.nn.sigmoid(value)
    return squash * (1.0 + value * (1.0 - squash))


def exchange(parts):
    return lax.all_to_all(parts, "table", split_axis=0, concat_axis=0, tiled=True)


def from_sibling(value):
    return lax.ppermute(value, "table", [(i, i ^ 1) for i in range(NT)])


def one_hot_rows(shape, source):
    row = lax.broadcasted_iota(jnp.int32, shape, 0)
    col = lax.broadcasted_iota(jnp.int32, shape, 1)
    return (source(row) == col).astype(F32).astype(BF)


def move_rows(order, rows):
    return jnp.dot(order, rows, preferred_element_type=F32).astype(BF)


def to_pieces(row):
    return ((row >> 1) & 3) * E + (row >> 3) * 2 + (row & 1)


def to_blocks(row):
    return ((row & 127) >> 1) * 8 + (row >> 7) * 2 + (row & 1)


def lift_kernel(got_ref, pooled_ref, u_ref, bias_ref, lifted_ref, factor_ref, terms_ref, weight_ref):
    weight = move_rows(one_hot_rows((512, 512), to_blocks), got_ref[:, 256:384])
    weight_ref[...] = weight
    factor = jnp.dot(got_ref[:, :256], u_ref[...], preferred_element_type=F32) + bias_ref[...] + 1.0
    factor_ref[...] = factor
    lifted = (pooled_ref[...].astype(F32) * factor).astype(BF)
    lifted_ref[...] = lifted
    for q in range(4):
        cols = slice(q * E, (q + 1) * E)
        terms_ref[:, cols] = jnp.dot(
            lifted[:, cols], weight[cols], preferred_element_type=F32
        ).astype(BF)


def whole(shape):
    return pl.BlockSpec(shape, lambda i: (0,) * len(shape))


def call(kernel, shapes, *values):
    return pl.pallas_call(
        kernel,
        grid=(1,),
        out_shape=[pltpu.HBM(shape.shape, shape.dtype) for shape in shapes],
        in_specs=[whole(value.shape) for value in values],
        out_specs=[whole(shape.shape) for shape in shapes],
        compiler_params=pltpu.CompilerParams(vmem_limit_bytes=24 * 1024 * 1024),
    )(*values)


def lift(got, pooled, cross_u, bias):
    shapes = [((512, 512), BF), ((512, 512), F32), ((512, 512), BF), ((512, E), BF)]
    return call(
        lift_kernel,
        [jax.ShapeDtypeStruct(*shape) for shape in shapes],
        got,
        pooled,
        cross_u,
        bias,
    )


def first_kernel(got_ref, adds_ref, bias_ref, preact_ref, hidden_ref):
    total = jnp.broadcast_to(bias_ref[...][:, None, :], (HB, 8, E)).reshape(HB * 8, E)
    for q in range(4):
        total = total + jnp.dot(
            adds_ref[q], got_ref[:, q * E : (q + 1) * E], preferred_element_type=F32
        )
    preact_ref[...] = total
    hidden_ref[...] = (total * jax.nn.sigmoid(total)).astype(BF)


def hidden_first(got, adds, bias):
    return call(
        first_kernel,
        [jax.ShapeDtypeStruct((HB * 8, E), F32), jax.ShapeDtypeStruct((HB * 8, E), BF)],
        got,
        adds,
        bias,
    )


def start_kernel(pooled_ref, v_ref, weight_ref, pair_ref, out_ref):
    out_ref[:, :256] = jnp.dot(
        pooled_ref[...], v_ref[...], preferred_element_type=F32
    ).astype(BF)
    out_ref[:, 256:384] = move_rows(one_hot_rows((512, 512), to_pieces), weight_ref[...])
    pair = pair_ref[...]
    for i in range(32):
        out_ref[16 * i : 16 * i + 16, 384:] = pair


def regroup_kernel(got_ref, index_ref, extra_ref, out_ref):
    own = jnp.sum(got_ref[:, :256].astype(F32).reshape(NT, 8, 256), axis=0)
    own = jnp.concatenate([own, extra_ref[...]], axis=1) if extra_ref is not None else own
    width = own.shape[1]
    out_ref[:, :width] = (
        jnp.broadcast_to(own[None], (NT, 8, width)).reshape(512, width).astype(BF)
    )
    row = lax.broadcasted_iota(jnp.int32, (512, 512), 0)
    col = lax.broadcasted_iota(jnp.int32, (512, 512), 1)
    order = (index_ref[...] == (col >> 1)) & ((row & 1) == (col & 1))
    out_ref[:, width:] = move_rows(order.astype(F32).astype(BF), got_ref[:, 256:384])


def regroup(got, index, extra=None):
    kernel = regroup_kernel if extra is not None else (
        lambda got_ref, index_ref, out_ref: regroup_kernel(got_ref, index_ref, None, out_ref)
    )
    values = (got, index) if extra is None else (got, index, extra)
    width = 384 if extra is None else 512
    return pl.pallas_call(
        kernel,
        grid=(1,),
        out_shape=pltpu.HBM((512, width), BF),
        in_specs=[pl.BlockSpec((512, 384), lambda i: (0, 0))]
        + [pl.BlockSpec(value.shape, lambda i: (0, 0)) for value in values[1:]],
        out_specs=pl.BlockSpec((512, width), lambda i: (0, 0)),
        compiler_params=pltpu.CompilerParams(vmem_limit_bytes=24 * 1024 * 1024),
    )(*values)


def contract(left, right, at):
    return lax.dot_general(left, right, (((at,), (at,)), ((), ())), preferred_element_type=F32)


def owner_kernel(
    got_ref,
    weight_ref,
    lifted_ref,
    pooled_ref,
    factor_ref,
    crossed_ref,
    u_ref,
    sent_ref,
    direct_ref,
    up_ref,
    two_ref,
    vector_ref,
    bias_ref,
):
    crossed = crossed_ref[:, :256]
    back = jnp.zeros((512, 256), F32)
    blocks = []
    bias_ref[...] = jnp.zeros_like(bias_ref)
    for q in range(4):
        cols = slice(q * E, (q + 1) * E)
        rows = got_ref[:, cols]
        lifted_grad = contract(rows, weight_ref[cols, :], 1).astype(BF).astype(F32)
        cross_grad = lifted_grad * pooled_ref[:, cols].astype(F32)
        cross_half = cross_grad.astype(BF)
        direct_ref[:, cols] = lifted_grad * factor_ref[:, cols]
        back = back + contract(cross_half, u_ref[:, cols], 1)
        blocks.append(contract(lifted_ref[:, cols], rows, 0).astype(BF))
        up_ref[:, cols] = contract(crossed, cross_half, 0).astype(BF)
        bias_ref[q : q + 1, :] = jnp.sum(cross_grad, axis=0, keepdims=True)
    sent_ref[:, :256] = back.astype(BF)
    sent_ref[:, 256:] = move_rows(
        one_hot_rows((512, 512), to_pieces), jnp.concatenate(blocks, axis=0)
    )
    two_rows = got_ref[:, 6 * E : 7 * E]
    two_ref[...] = contract(got_ref[:, 4 * E : 6 * E], two_rows, 0).astype(BF)
    vector_ref[...] = jnp.concatenate(
        [
            jnp.sum(two_rows.astype(F32), axis=0, keepdims=True),
            jnp.sum(got_ref[:, 7 * E :].astype(F32), axis=0, keepdims=True),
            jnp.zeros((6, E), F32),
        ],
        axis=0,
    )


QUARTER = 368


def late_kernel(got_ref, pooled_ref, up_ref, two_ref, bias_ref, late_ref):
    local_v = contract(pooled_ref[...], got_ref[:, :256], 0).astype(BF)
    blocks = move_rows(one_hot_rows((512, 512), to_blocks), got_ref[:, 384:])

    def vector_source(row):
        place = (row >> 5) * 24 + (row & 31)
        which = place >> 5
        hidden = place & 31
        return 16 * hidden + jnp.where(which == 2, 8, 0) + jnp.where(which == 1, 0, 1)

    order = one_hot_rows((E, 512), vector_source)
    vectors = jnp.dot(order, got_ref[:, 256:384], preferred_element_type=F32)
    in_quarter = lax.broadcasted_iota(jnp.int32, (32, E), 0)
    for k in range(4):
        base = QUARTER * k
        late_ref[base : base + 128, :] = local_v[128 * k : 128 * k + 128]
        small = vectors[32 * k : 32 * k + 32]
        small = jnp.where(in_quarter == 24, bias_ref[k : k + 1, :], small).astype(BF)
        for side in range(2):
            cols = slice(side * E, (side + 1) * E)
            at = 128 * k + 64 * side
            late_ref[base + 128 : base + 192, cols] = blocks[at : at + 64]
            late_ref[base + 192 : base + 208, cols] = small[16 * side : 16 * side + 16]
            at = base + 208 + 64 * side
            late_ref[at : at + 64, :] = up_ref[64 * k : 64 * k + 64, 256 * side : 256 * side + 256]
            at = 64 * k + 32 * side
            late_ref[base + 336 : base + 368, cols] = two_ref[at : at + 32, :]


def add_kernel(got_ref, out_ref):
    total = got_ref[:QUARTER, :].astype(F32)
    for k in range(1, 4):
        total = total + got_ref[QUARTER * k : QUARTER * (k + 1), :].astype(F32)
    for k in range(4):
        out_ref[QUARTER * k : QUARTER * (k + 1), :] = total.astype(BF)


def last_kernel(got_ref, v_ref, one_ref, small_ref, up_ref, two_ref):
    for k in range(4):
        base = QUARTER * k
        v_ref[128 * k : 128 * k + 128, :] = got_ref[base : base + 128, :].astype(F32)
        for side in range(2):
            cols = slice(side * E, (side + 1) * E)
            at = 128 * k + 64 * side
            one_ref[at : at + 64, :] = got_ref[base + 128 : base + 192, cols].astype(F32)
            at = 32 * k + 16 * side
            small_ref[at : at + 16, :] = got_ref[base + 192 : base + 208, cols].astype(F32)
            at = base + 208 + 64 * side
            up_ref[64 * k : 64 * k + 64, 256 * side : 256 * side + 256] = got_ref[
                at : at + 64, :
            ].astype(F32)
            at = 64 * k + 32 * side
            two_ref[at : at + 32, :] = got_ref[base + 336 : base + 368, cols].astype(F32)


def body(
    pooled,
    table_slot,
    cross_v,
    cross_u,
    cross_bias,
    block_index1,
    weight1,
    block_index2,
    weight2,
    top_vectors,
    labels,
    importance,
):
    tables = table_slot.shape[0]
    contract_last = (((1,), (1,)), ((), ()))
    core = lax.axis_index("table") % 2
    half_index = lax.dynamic_index_in_dim(block_index2.reshape(HB, 2, 2), core, 2, keepdims=False)
    half_index = half_index.reshape(-1)

    reads = block_index1[:, None] == table_slot[None, :]
    numbers = jnp.arange(tables, dtype=jnp.int32)
    block_of_slot = jnp.sum(jnp.where(reads, numbers[:, None], 0), axis=0)
    slot_of_block = jnp.sum(jnp.where(reads, numbers[None, :], 0), axis=1)
    block_of_slot = jnp.repeat(block_of_slot, 2)[:, None]
    slot_of_block = jnp.repeat(slot_of_block, 2)[:, None]
    hidden_of_slot = jnp.sum(
        jnp.where(reads, jnp.arange(tables, dtype=jnp.int32)[:, None] // K1, 0), axis=0
    )
    out_row = lax.broadcasted_iota(jnp.int32, (4, HB * 8, NT * 8), 1)
    in_row = lax.broadcasted_iota(jnp.int32, (4, HB * 8, NT * 8), 2)
    wanted = jnp.repeat(hidden_of_slot.reshape(NT, 4).T, 8, axis=1)[:, None, :]
    adds = ((wanted == out_row // 8) & (out_row % 8 == in_row % 8)).astype(BF)

    pair_two = weight2.reshape(2, 16, 8, E).transpose(0, 2, 1, 3).reshape(16, 16 * E)
    (sent,) = call(
        start_kernel,
        [jax.ShapeDtypeStruct((512, 2432), BF)],
        pooled,
        cross_v,
        weight1.reshape(512, E),
        pair_two,
    )
    got = exchange(sent.reshape(NT, 8, 2432))
    half_two = got[:, :, 384:].reshape(NT, 8, 16, E).transpose(0, 2, 1, 3).reshape(NT, E, E)
    sent = regroup(got.reshape(512, 2432), block_of_slot)
    arrived = exchange(sent.reshape(NT, 8, 384)).reshape(512, 384)
    lifted, factor, terms, weight_slot = lift(
        arrived, pooled, cross_u, cross_bias.reshape(1, 512)
    )
    got = exchange(terms.reshape(NT, 8, 512))
    preact_one, hidden_one = hidden_first(
        got.reshape(512, 512), adds, top_vectors[0].reshape(HB, E)
    )
    preact_one = preact_one.reshape(HB, 8, E).transpose(1, 0, 2)
    hidden_one = hidden_one.reshape(HB, 8, E).transpose(1, 0, 2)
    hidden_both = jnp.concatenate([hidden_one, from_sibling(hidden_one)], axis=0)
    picked_both = hidden_both[:, half_index]
    terms_two = jnp.einsum("bnc,ncd->bnd", picked_both, half_two, preferred_element_type=F32)
    half_sum = terms_two.reshape(16, HB, 2, E).sum(axis=2)
    preact_two = half_sum[:8] + from_sibling(half_sum[8:]) + top_vectors[1].reshape(-1, E)
    hidden_two = jax.nn.silu(preact_two).astype(BF)
    last_weight = top_vectors[2].reshape(-1, E)
    logit = jnp.sum(hidden_two.astype(F32) * last_weight, axis=(1, 2))
    sample_weight = importance.reshape(-1).astype(F32) / 8.0
    targets = labels.reshape(-1).astype(F32)
    grad_logit = sample_weight * (jax.nn.sigmoid(logit) - targets)
    grad_two = (grad_logit[:, None, None] * last_weight * silu_slope(preact_two)).astype(BF)
    last_terms = (hidden_two.astype(F32) * grad_logit[:, None, None]).astype(BF)
    grad_both = jnp.concatenate([grad_two, from_sibling(grad_two)], axis=0)
    spread_two = jnp.repeat(grad_both, 2, axis=1)
    back_two = jnp.einsum("bnd,ncd->bnc", spread_two, half_two, preferred_element_type=F32)
    onehot_two = (half_index[:, None] == jnp.arange(HB, dtype=jnp.int32)[None, :]).astype(F32)
    half_into = jnp.einsum("bnc,nj->bjc", back_two, onehot_two, precision=lax.Precision.HIGHEST)
    into_one = half_into[:8] + from_sibling(half_into[8:])
    grad_one = (into_one * silu_slope(preact_one)).astype(BF)

    spread_one = grad_one[:, hidden_of_slot].reshape(8, NT, 4 * E)
    picked_pair = hidden_one[:, block_index2].reshape(8, NT, 2 * E)
    both = jnp.repeat(grad_two, 2, axis=1)
    third = jnp.stack([grad_one, last_terms], axis=2).reshape(8, NT, E)
    sent = jnp.concatenate([spread_one, picked_pair, both, third], axis=2).transpose(1, 0, 2)
    got = exchange(sent).reshape(512, 8 * E)
    sent, direct, local_u, local_two, vector_rows, local_bias = call(
        owner_kernel,
        [
            jax.ShapeDtypeStruct((512, 384), BF),
            jax.ShapeDtypeStruct((512, 512), F32),
            jax.ShapeDtypeStruct((256, 512), BF),
            jax.ShapeDtypeStruct((256, E), BF),
            jax.ShapeDtypeStruct((8, E), F32),
            jax.ShapeDtypeStruct((8, E), F32),
        ],
        got,
        weight_slot,
        lifted,
        pooled,
        factor,
        arrived,
        cross_u,
    )
    got = exchange(sent.reshape(NT, 8, 384))
    sent = regroup(got.reshape(512, 384), slot_of_block, vector_rows)
    got = exchange(sent.reshape(NT, 8, 512)).reshape(512, 512)
    grad_crossed = got[:, :256]
    parts = [jax.ShapeDtypeStruct((4 * QUARTER, 256), BF)]
    (late,) = call(late_kernel, parts, got, pooled, local_u, local_two, local_bias)
    late = lax.all_to_all(late, "rep", split_axis=0, concat_axis=0, tiled=True)
    (late,) = call(add_kernel, parts, late)
    late = lax.all_to_all(late, "rep", split_axis=0, concat_axis=0, tiled=True)
    shapes = [(512, 256), (512, E), (E, E), (256, 512), (256, E)]
    grad_v, grad_w1, small, grad_u, grad_w2 = call(
        last_kernel, [jax.ShapeDtypeStruct(shape, F32) for shape in shapes], late
    )
    d_pooled = (
        direct + lax.dot_general(grad_crossed, cross_v, contract_last, preferred_element_type=F32)
    ).astype(BF)

    grad_w1 = grad_w1.reshape(4, E, E)
    grad_w2 = grad_w2.reshape(2, E, E)
    small = small.reshape(4, 32, E)
    grad_bias = small[:, 24].reshape(512)
    grad_vectors = small[:, :24].reshape(3, HB * E)
    return (d_pooled, grad_v, grad_u, grad_bias, grad_w1, grad_w2, grad_vectors)


def solution(mesh):
    placed = (
        P("rep", "table"),
        P(),
        P("table", None),
        P(None, "table"),
        P("table"),
        P(),
        P("table", None, None),
        P(),
        P("table", None, None),
        P(),
        P("rep", "table"),
        P("rep", "table"),
    )
    return jax.shard_map(
        body,
        mesh=mesh,
        in_specs=placed,
        out_specs=(
            P("rep", "table"),
            P("table", None),
            P(None, "table"),
            P("table"),
            P("table", None, None),
            P("table", None, None),
            P(),
        ),
        check_vma=False,
    )
```

```python
import jax
import jax.numpy as jnp
from jax import lax
from jax.experimental import pallas as pl
from jax.experimental.pallas import tpu as pltpu
from jax.sharding import PartitionSpec as P

E = 128
K1 = 8
K2 = 4
HB = 32
NT = 64
N_REP = 4
BF = jnp.bfloat16
F32 = jnp.float32


def silu_slope(value):
    squash = jax.nn.sigmoid(value)
    return squash * (1.0 + value * (1.0 - squash))


def exchange(parts):
    return lax.all_to_all(parts, "table", split_axis=0, concat_axis=0, tiled=True)


def from_sibling(value):
    return lax.ppermute(value, "table", [(i, i ^ 1) for i in range(NT)])


def one_hot_rows(shape, source):
    row = lax.broadcasted_iota(jnp.int32, shape, 0)
    col = lax.broadcasted_iota(jnp.int32, shape, 1)
    return (source(row) == col).astype(F32).astype(BF)


def move_rows(order, rows):
    return jnp.dot(order, rows, preferred_element_type=F32).astype(BF)


def to_pieces(row):
    return ((row >> 1) & 3) * E + (row >> 3) * 2 + (row & 1)


def to_blocks(row):
    return ((row & 127) >> 1) * 8 + (row >> 7) * 2 + (row & 1)


def lift_kernel(got_ref, pooled_ref, u_ref, bias_ref, lifted_ref, factor_ref, terms_ref, weight_ref):
    weight = move_rows(one_hot_rows((512, 512), to_blocks), got_ref[:, 256:384])
    weight_ref[...] = weight
    factor = jnp.dot(got_ref[:, :256], u_ref[...], preferred_element_type=F32) + bias_ref[...] + 1.0
    factor_ref[...] = factor
    lifted = (pooled_ref[...].astype(F32) * factor).astype(BF)
    lifted_ref[...] = lifted
    for q in range(4):
        cols = slice(q * E, (q + 1) * E)
        terms_ref[:, cols] = jnp.dot(
            lifted[:, cols], weight[cols], preferred_element_type=F32
        ).astype(BF)


def whole(shape):
    return pl.BlockSpec(shape, lambda i: (0,) * len(shape))


def call(kernel, shapes, *values):
    return pl.pallas_call(
        kernel,
        grid=(1,),
        out_shape=[pltpu.HBM(shape.shape, shape.dtype) for shape in shapes],
        in_specs=[whole(value.shape) for value in values],
        out_specs=[whole(shape.shape) for shape in shapes],
        compiler_params=pltpu.CompilerParams(vmem_limit_bytes=24 * 1024 * 1024),
    )(*values)


def lift(got, pooled, cross_u, bias):
    shapes = [((512, 512), BF), ((512, 512), F32), ((512, 512), BF), ((512, E), BF)]
    return call(
        lift_kernel,
        [jax.ShapeDtypeStruct(*shape) for shape in shapes],
        got,
        pooled,
        cross_u,
        bias,
    )


def first_kernel(got_ref, adds_ref, bias_ref, preact_ref, hidden_ref):
    total = jnp.broadcast_to(bias_ref[...][:, None, :], (HB, 8, E)).reshape(HB * 8, E)
    for q in range(4):
        total = total + jnp.dot(
            adds_ref[q], got_ref[:, q * E : (q + 1) * E], preferred_element_type=F32
        )
    preact_ref[...] = total
    hidden_ref[...] = (total * jax.nn.sigmoid(total)).astype(BF)


def hidden_first(got, adds, bias):
    return call(
        first_kernel,
        [jax.ShapeDtypeStruct((HB * 8, E), F32), jax.ShapeDtypeStruct((HB * 8, E), BF)],
        got,
        adds,
        bias,
    )


def start_kernel(pooled_ref, v_ref, weight_ref, pair_ref, out_ref):
    out_ref[:, :256] = jnp.dot(
        pooled_ref[...], v_ref[...], preferred_element_type=F32
    ).astype(BF)
    out_ref[:, 256:384] = move_rows(one_hot_rows((512, 512), to_pieces), weight_ref[...])
    pair = pair_ref[...]
    for i in range(32):
        out_ref[16 * i : 16 * i + 16, 384:] = pair


def regroup_kernel(got_ref, index_ref, extra_ref, out_ref):
    own = jnp.sum(got_ref[:, :256].astype(F32).reshape(NT, 8, 256), axis=0)
    own = jnp.concatenate([own, extra_ref[...]], axis=1) if extra_ref is not None else own
    width = own.shape[1]
    out_ref[:, :width] = (
        jnp.broadcast_to(own[None], (NT, 8, width)).reshape(512, width).astype(BF)
    )
    row = lax.broadcasted_iota(jnp.int32, (512, 512), 0)
    col = lax.broadcasted_iota(jnp.int32, (512, 512), 1)
    order = (index_ref[...] == (col >> 1)) & ((row & 1) == (col & 1))
    out_ref[:, width:] = move_rows(order.astype(F32).astype(BF), got_ref[:, 256:384])


def regroup(got, index, extra=None):
    kernel = regroup_kernel if extra is not None else (
        lambda got_ref, index_ref, out_ref: regroup_kernel(got_ref, index_ref, None, out_ref)
    )
    values = (got, index) if extra is None else (got, index, extra)
    width = 384 if extra is None else 512
    return pl.pallas_call(
        kernel,
        grid=(1,),
        out_shape=pltpu.HBM((512, width), BF),
        in_specs=[pl.BlockSpec((512, 384), lambda i: (0, 0))]
        + [pl.BlockSpec(value.shape, lambda i: (0, 0)) for value in values[1:]],
        out_specs=pl.BlockSpec((512, width), lambda i: (0, 0)),
        compiler_params=pltpu.CompilerParams(vmem_limit_bytes=24 * 1024 * 1024),
    )(*values)


def contract(left, right, at):
    return lax.dot_general(left, right, (((at,), (at,)), ((), ())), preferred_element_type=F32)


def factors_kernel(
    own_ref, far_ref, preact_ref, adds_ref, picks_ref, hidden_ref, two_ref, terms_ref, out_ref
):
    grad_one = ((own_ref[...] + far_ref[...]) * silu_slope(preact_ref[...])).astype(BF)
    for q in range(4):
        out_ref[:, q * E : (q + 1) * E] = contract(adds_ref[q], grad_one, 0).astype(BF)
    hidden = hidden_ref[...]
    for e in range(2):
        out_ref[:, (4 + e) * E : (5 + e) * E] = contract(picks_ref[e], hidden, 0).astype(BF)
    order = one_hot_rows((512, 256), lambda row: (row >> 4) * 8 + (row & 7))
    out_ref[:, 6 * E : 7 * E] = move_rows(order, two_ref[...])
    row = lax.broadcasted_iota(jnp.int32, (512, E), 0)
    out_ref[:, 7 * E :] = jnp.where(
        ((row >> 3) & 1) == 0,
        jnp.dot(order, grad_one, preferred_element_type=F32),
        jnp.dot(order, terms_ref[...], preferred_element_type=F32),
    ).astype(BF)


def owner_kernel(
    got_ref,
    weight_ref,
    lifted_ref,
    pooled_ref,
    factor_ref,
    crossed_ref,
    u_ref,
    sent_ref,
    direct_ref,
    up_ref,
    two_ref,
    vector_ref,
    bias_ref,
):
    crossed = crossed_ref[:, :256]
    back = jnp.zeros((512, 256), F32)
    blocks = []
    bias_ref[...] = jnp.zeros_like(bias_ref)
    for q in range(4):
        cols = slice(q * E, (q + 1) * E)
        rows = got_ref[:, cols]
        lifted_grad = contract(rows, weight_ref[cols, :], 1).astype(BF).astype(F32)
        cross_grad = lifted_grad * pooled_ref[:, cols].astype(F32)
        cross_half = cross_grad.astype(BF)
        direct_ref[:, cols] = lifted_grad * factor_ref[:, cols]
        back = back + contract(cross_half, u_ref[:, cols], 1)
        blocks.append(contract(lifted_ref[:, cols], rows, 0).astype(BF))
        up_ref[:, cols] = contract(crossed, cross_half, 0).astype(BF)
        bias_ref[q : q + 1, :] = jnp.sum(cross_grad, axis=0, keepdims=True)
    sent_ref[:, :256] = back.astype(BF)
    sent_ref[:, 256:] = move_rows(
        one_hot_rows((512, 512), to_pieces), jnp.concatenate(blocks, axis=0)
    )
    two_rows = got_ref[:, 6 * E : 7 * E]
    two_ref[...] = contract(got_ref[:, 4 * E : 6 * E], two_rows, 0).astype(BF)
    vector_ref[...] = jnp.concatenate(
        [
            jnp.sum(two_rows.astype(F32), axis=0, keepdims=True),
            jnp.sum(got_ref[:, 7 * E :].astype(F32), axis=0, keepdims=True),
            jnp.zeros((6, E), F32),
        ],
        axis=0,
    )


QUARTER = 368


def late_kernel(got_ref, pooled_ref, up_ref, two_ref, bias_ref, late_ref):
    local_v = contract(pooled_ref[...], got_ref[:, :256], 0).astype(BF)
    blocks = move_rows(one_hot_rows((512, 512), to_blocks), got_ref[:, 384:])

    def vector_source(row):
        place = (row >> 5) * 24 + (row & 31)
        which = place >> 5
        hidden = place & 31
        return 16 * hidden + jnp.where(which == 2, 8, 0) + jnp.where(which == 1, 0, 1)

    order = one_hot_rows((E, 512), vector_source)
    vectors = jnp.dot(order, got_ref[:, 256:384], preferred_element_type=F32)
    in_quarter = lax.broadcasted_iota(jnp.int32, (32, E), 0)
    for k in range(4):
        base = QUARTER * k
        late_ref[base : base + 128, :] = local_v[128 * k : 128 * k + 128]
        small = vectors[32 * k : 32 * k + 32]
        small = jnp.where(in_quarter == 24, bias_ref[k : k + 1, :], small).astype(BF)
        for side in range(2):
            cols = slice(side * E, (side + 1) * E)
            at = 128 * k + 64 * side
            late_ref[base + 128 : base + 192, cols] = blocks[at : at + 64]
            late_ref[base + 192 : base + 208, cols] = small[16 * side : 16 * side + 16]
            at = base + 208 + 64 * side
            late_ref[at : at + 64, :] = up_ref[64 * k : 64 * k + 64, 256 * side : 256 * side + 256]
            at = 64 * k + 32 * side
            late_ref[base + 336 : base + 368, cols] = two_ref[at : at + 32, :]


def add_kernel(got_ref, out_ref):
    total = got_ref[:QUARTER, :].astype(F32)
    for k in range(1, 4):
        total = total + got_ref[QUARTER * k : QUARTER * (k + 1), :].astype(F32)
    for k in range(4):
        out_ref[QUARTER * k : QUARTER * (k + 1), :] = total.astype(BF)


def last_kernel(got_ref, v_ref, one_ref, small_ref, up_ref, two_ref):
    for k in range(4):
        base = QUARTER * k
        v_ref[128 * k : 128 * k + 128, :] = got_ref[base : base + 128, :].astype(F32)
        for side in range(2):
            cols = slice(side * E, (side + 1) * E)
            at = 128 * k + 64 * side
            one_ref[at : at + 64, :] = got_ref[base + 128 : base + 192, cols].astype(F32)
            at = 32 * k + 16 * side
            small_ref[at : at + 16, :] = got_ref[base + 192 : base + 208, cols].astype(F32)
            at = base + 208 + 64 * side
            up_ref[64 * k : 64 * k + 64, 256 * side : 256 * side + 256] = got_ref[
                at : at + 64, :
            ].astype(F32)
            at = 64 * k + 32 * side
            two_ref[at : at + 32, :] = got_ref[base + 336 : base + 368, cols].astype(F32)


def body(
    pooled,
    table_slot,
    cross_v,
    cross_u,
    cross_bias,
    block_index1,
    weight1,
    block_index2,
    weight2,
    top_vectors,
    labels,
    importance,
):
    tables = table_slot.shape[0]
    contract_last = (((1,), (1,)), ((), ()))
    core = lax.axis_index("table") % 2
    half_index = lax.dynamic_index_in_dim(block_index2.reshape(HB, 2, 2), core, 2, keepdims=False)
    half_index = half_index.reshape(-1)

    reads = block_index1[:, None] == table_slot[None, :]
    numbers = jnp.arange(tables, dtype=jnp.int32)
    block_of_slot = jnp.sum(jnp.where(reads, numbers[:, None], 0), axis=0)
    slot_of_block = jnp.sum(jnp.where(reads, numbers[None, :], 0), axis=1)
    block_of_slot = jnp.repeat(block_of_slot, 2)[:, None]
    slot_of_block = jnp.repeat(slot_of_block, 2)[:, None]
    hidden_of_slot = jnp.sum(
        jnp.where(reads, jnp.arange(tables, dtype=jnp.int32)[:, None] // K1, 0), axis=0
    )
    def spread(blocks):
        shape = (blocks.shape[1], HB * 8, NT * 8)
        out_row = lax.broadcasted_iota(jnp.int32, shape, 1)
        in_row = lax.broadcasted_iota(jnp.int32, shape, 2)
        wanted = jnp.repeat(blocks.T, 8, axis=1)[:, None, :]
        return ((wanted == out_row // 8) & (out_row % 8 == in_row % 8)).astype(BF)

    adds = spread(hidden_of_slot.reshape(NT, 4))
    picks = spread(block_index2.reshape(NT, 2))

    pair_two = weight2.reshape(2, 16, 8, E).transpose(0, 2, 1, 3).reshape(16, 16 * E)
    (sent,) = call(
        start_kernel,
        [jax.ShapeDtypeStruct((512, 2432), BF)],
        pooled,
        cross_v,
        weight1.reshape(512, E),
        pair_two,
    )
    got = exchange(sent.reshape(NT, 8, 2432))
    half_two = got[:, :, 384:].reshape(NT, 8, 16, E).transpose(0, 2, 1, 3).reshape(NT, E, E)
    sent = regroup(got.reshape(512, 2432), block_of_slot)
    arrived = exchange(sent.reshape(NT, 8, 384)).reshape(512, 384)
    lifted, factor, terms, weight_slot = lift(
        arrived, pooled, cross_u, cross_bias.reshape(1, 512)
    )
    got = exchange(terms.reshape(NT, 8, 512))
    preact_one, hidden_one = hidden_first(
        got.reshape(512, 512), adds, top_vectors[0].reshape(HB, E)
    )
    def with_sibling(rows):
        return jnp.concatenate(
            [rows.reshape(HB, 8, E), from_sibling(rows).reshape(HB, 8, E)], axis=1
        )

    picked_both = with_sibling(hidden_one)[half_index]
    terms_two = jnp.einsum("nbc,ncd->nbd", picked_both, half_two, preferred_element_type=F32)
    half_sum = terms_two.reshape(HB, 2, 16, E).sum(axis=1)
    preact_two = half_sum[:, :8] + from_sibling(half_sum[:, 8:])
    preact_two = preact_two + top_vectors[1].reshape(HB, 1, E)
    hidden_two = jax.nn.silu(preact_two).astype(BF).astype(F32)
    last_weight = top_vectors[2].reshape(HB, 1, E)
    logit = jnp.sum(hidden_two * last_weight, axis=(0, 2))
    sample_weight = importance.reshape(-1).astype(F32) / 8.0
    grad_logit = sample_weight * (jax.nn.sigmoid(logit) - labels.reshape(-1).astype(F32))
    grad_logit = grad_logit[None, :, None]
    grad_two = (grad_logit * last_weight * silu_slope(preact_two)).astype(BF)
    grad_two = grad_two.reshape(HB * 8, E)
    last_terms = (hidden_two * grad_logit).astype(BF).reshape(HB * 8, E)
    spread_two = jnp.repeat(with_sibling(grad_two), 2, axis=0)
    back_two = jnp.einsum("nbd,ncd->nbc", spread_two, half_two, preferred_element_type=F32)
    onehot_two = (jnp.arange(HB, dtype=jnp.int32)[:, None] == half_index[None, :]).astype(F32)
    half_into = jnp.einsum("jn,nbc->jbc", onehot_two, back_two, precision=lax.Precision.HIGHEST)

    (sent,) = call(
        factors_kernel,
        [jax.ShapeDtypeStruct((512, 8 * E), BF)],
        half_into[:, :8].reshape(HB * 8, E),
        from_sibling(half_into[:, 8:].reshape(HB * 8, E)),
        preact_one,
        adds,
        picks,
        hidden_one,
        grad_two,
        last_terms,
    )
    got = exchange(sent.reshape(NT, 8, 8 * E)).reshape(512, 8 * E)
    sent, direct, local_u, local_two, vector_rows, local_bias = call(
        owner_kernel,
        [
            jax.ShapeDtypeStruct((512, 384), BF),
            jax.ShapeDtypeStruct((512, 512), F32),
            jax.ShapeDtypeStruct((256, 512), BF),
            jax.ShapeDtypeStruct((256, E), BF),
            jax.ShapeDtypeStruct((8, E), F32),
            jax.ShapeDtypeStruct((8, E), F32),
        ],
        got,
        weight_slot,
        lifted,
        pooled,
        factor,
        arrived,
        cross_u,
    )
    got = exchange(sent.reshape(NT, 8, 384))
    sent = regroup(got.reshape(512, 384), slot_of_block, vector_rows)
    got = exchange(sent.reshape(NT, 8, 512)).reshape(512, 512)
    grad_crossed = got[:, :256]
    parts = [jax.ShapeDtypeStruct((4 * QUARTER, 256), BF)]
    (late,) = call(late_kernel, parts, got, pooled, local_u, local_two, local_bias)
    late = lax.all_to_all(late, "rep", split_axis=0, concat_axis=0, tiled=True)
    (late,) = call(add_kernel, parts, late)
    late = lax.all_to_all(late, "rep", split_axis=0, concat_axis=0, tiled=True)
    shapes = [(512, 256), (512, E), (E, E), (256, 512), (256, E)]
    grad_v, grad_w1, small, grad_u, grad_w2 = call(
        last_kernel, [jax.ShapeDtypeStruct(shape, F32) for shape in shapes], late
    )
    d_pooled = (
        direct + lax.dot_general(grad_crossed, cross_v, contract_last, preferred_element_type=F32)
    ).astype(BF)

    grad_w1 = grad_w1.reshape(4, E, E)
    grad_w2 = grad_w2.reshape(2, E, E)
    small = small.reshape(4, 32, E)
    grad_bias = small[:, 24].reshape(512)
    grad_vectors = small[:, :24].reshape(3, HB * E)
    return (d_pooled, grad_v, grad_u, grad_bias, grad_w1, grad_w2, grad_vectors)


def solution(mesh):
    placed = (
        P("rep", "table"),
        P(),
        P("table", None),
        P(None, "table"),
        P("table"),
        P(),
        P("table", None, None),
        P(),
        P("table", None, None),
        P(),
        P("rep", "table"),
        P("rep", "table"),
    )
    return jax.shard_map(
        body,
        mesh=mesh,
        in_specs=placed,
        out_specs=(
            P("rep", "table"),
            P("table", None),
            P(None, "table"),
            P("table"),
            P("table", None, None),
            P("table", None, None),
            P(),
        ),
        check_vma=False,
    )
```

```python
import jax
import jax.numpy as jnp
from jax import lax
from jax.experimental import pallas as pl
from jax.experimental.pallas import tpu as pltpu
from jax.sharding import PartitionSpec as P

E = 128
K1 = 8
K2 = 4
HB = 32
NT = 64
N_REP = 4
BF = jnp.bfloat16
F32 = jnp.float32


def silu_slope(value):
    squash = jax.nn.sigmoid(value)
    return squash * (1.0 + value * (1.0 - squash))


def exchange(parts):
    return lax.all_to_all(parts, "table", split_axis=0, concat_axis=0, tiled=True)


def from_sibling(value):
    return lax.ppermute(value, "table", [(i, i ^ 1) for i in range(NT)])


def one_hot_rows(shape, source):
    row = lax.broadcasted_iota(jnp.int32, shape, 0)
    col = lax.broadcasted_iota(jnp.int32, shape, 1)
    return (source(row) == col).astype(F32).astype(BF)


def move_rows(order, rows):
    return jnp.dot(order, rows, preferred_element_type=F32).astype(BF)


def to_pieces(row):
    return ((row >> 1) & 3) * E + (row >> 3) * 2 + (row & 1)


def to_blocks(row):
    return ((row & 127) >> 1) * 8 + (row >> 7) * 2 + (row & 1)


def lift_kernel(got_ref, pooled_ref, u_ref, bias_ref, lifted_ref, factor_ref, terms_ref, weight_ref):
    weight = move_rows(one_hot_rows((512, 512), to_blocks), got_ref[:, 256:384])
    weight_ref[...] = weight
    factor = jnp.dot(got_ref[:, :256], u_ref[...], preferred_element_type=F32) + bias_ref[...] + 1.0
    factor_ref[...] = factor
    lifted = (pooled_ref[...].astype(F32) * factor).astype(BF)
    lifted_ref[...] = lifted
    for q in range(4):
        cols = slice(q * E, (q + 1) * E)
        terms_ref[:, cols] = jnp.dot(
            lifted[:, cols], weight[cols], preferred_element_type=F32
        ).astype(BF)


def whole(shape):
    return pl.BlockSpec(shape, lambda i: (0,) * len(shape))


def call(kernel, shapes, *values):
    return pl.pallas_call(
        kernel,
        grid=(1,),
        out_shape=[pltpu.HBM(shape.shape, shape.dtype) for shape in shapes],
        in_specs=[whole(value.shape) for value in values],
        out_specs=[whole(shape.shape) for shape in shapes],
        compiler_params=pltpu.CompilerParams(vmem_limit_bytes=24 * 1024 * 1024),
    )(*values)


def lift(got, pooled, cross_u, bias):
    shapes = [((512, 512), BF), ((512, 512), F32), ((512, 512), BF), ((512, E), BF)]
    return call(
        lift_kernel,
        [jax.ShapeDtypeStruct(*shape) for shape in shapes],
        got,
        pooled,
        cross_u,
        bias,
    )


def first_kernel(got_ref, adds_ref, bias_ref, preact_ref, hidden_ref):
    total = jnp.broadcast_to(bias_ref[...][:, None, :], (HB, 8, E)).reshape(HB * 8, E)
    for q in range(4):
        total = total + jnp.dot(
            adds_ref[q], got_ref[:, q * E : (q + 1) * E], preferred_element_type=F32
        )
    preact_ref[...] = total
    hidden_ref[...] = (total * jax.nn.sigmoid(total)).astype(BF)


def hidden_first(got, adds, bias):
    return call(
        first_kernel,
        [jax.ShapeDtypeStruct((HB * 8, E), F32), jax.ShapeDtypeStruct((HB * 8, E), BF)],
        got,
        adds,
        bias,
    )


def start_kernel(pooled_ref, v_ref, weight_ref, out_ref):
    out_ref[:, :256] = jnp.dot(
        pooled_ref[...], v_ref[...], preferred_element_type=F32
    ).astype(BF)
    out_ref[:, 256:384] = move_rows(one_hot_rows((512, 512), to_pieces), weight_ref[...])


def regroup_kernel(got_ref, index_ref, extra_ref, out_ref):
    own = jnp.sum(got_ref[:, :256].astype(F32).reshape(NT, 8, 256), axis=0)
    own = jnp.concatenate([own, extra_ref[...]], axis=1) if extra_ref is not None else own
    width = own.shape[1]
    out_ref[:, :width] = (
        jnp.broadcast_to(own[None], (NT, 8, width)).reshape(512, width).astype(BF)
    )
    row = lax.broadcasted_iota(jnp.int32, (512, 512), 0)
    col = lax.broadcasted_iota(jnp.int32, (512, 512), 1)
    order = (index_ref[...] == (col >> 1)) & ((row & 1) == (col & 1))
    out_ref[:, width:] = move_rows(order.astype(F32).astype(BF), got_ref[:, 256:384])


def regroup(got, index, extra=None):
    kernel = regroup_kernel if extra is not None else (
        lambda got_ref, index_ref, out_ref: regroup_kernel(got_ref, index_ref, None, out_ref)
    )
    values = (got, index) if extra is None else (got, index, extra)
    width = 384 if extra is None else 512
    return pl.pallas_call(
        kernel,
        grid=(1,),
        out_shape=pltpu.HBM((512, width), BF),
        in_specs=[pl.BlockSpec((512, 384), lambda i: (0, 0))]
        + [pl.BlockSpec(value.shape, lambda i: (0, 0)) for value in values[1:]],
        out_specs=pl.BlockSpec((512, width), lambda i: (0, 0)),
        compiler_params=pltpu.CompilerParams(vmem_limit_bytes=24 * 1024 * 1024),
    )(*values)


def contract(left, right, at):
    return lax.dot_general(left, right, (((at,), (at,)), ((), ())), preferred_element_type=F32)


def owner_kernel(
    got_ref,
    weight_ref,
    lifted_ref,
    pooled_ref,
    factor_ref,
    crossed_ref,
    u_ref,
    sent_ref,
    direct_ref,
    up_ref,
    two_ref,
    vector_ref,
    bias_ref,
):
    crossed = crossed_ref[:, :256]
    back = jnp.zeros((512, 256), F32)
    blocks = []
    bias_ref[...] = jnp.zeros_like(bias_ref)
    for q in range(4):
        cols = slice(q * E, (q + 1) * E)
        rows = got_ref[:, cols]
        lifted_grad = contract(rows, weight_ref[cols, :], 1).astype(BF).astype(F32)
        cross_grad = lifted_grad * pooled_ref[:, cols].astype(F32)
        cross_half = cross_grad.astype(BF)
        direct_ref[:, cols] = lifted_grad * factor_ref[:, cols]
        back = back + contract(cross_half, u_ref[:, cols], 1)
        blocks.append(contract(lifted_ref[:, cols], rows, 0).astype(BF))
        up_ref[:, cols] = contract(crossed, cross_half, 0).astype(BF)
        bias_ref[q : q + 1, :] = jnp.sum(cross_grad, axis=0, keepdims=True)
    sent_ref[:, :256] = back.astype(BF)
    sent_ref[:, 256:] = move_rows(
        one_hot_rows((512, 512), to_pieces), jnp.concatenate(blocks, axis=0)
    )
    two_rows = got_ref[:, 6 * E : 7 * E]
    two_ref[...] = contract(got_ref[:, 4 * E : 6 * E], two_rows, 0).astype(BF)
    vector_ref[...] = jnp.concatenate(
        [
            jnp.sum(two_rows.astype(F32), axis=0, keepdims=True),
            jnp.sum(got_ref[:, 7 * E :].astype(F32), axis=0, keepdims=True),
            jnp.zeros((6, E), F32),
        ],
        axis=0,
    )


QUARTER = 368


def late_kernel(got_ref, pooled_ref, up_ref, two_ref, bias_ref, late_ref):
    local_v = contract(pooled_ref[...], got_ref[:, :256], 0).astype(BF)
    blocks = move_rows(one_hot_rows((512, 512), to_blocks), got_ref[:, 384:])

    def vector_source(row):
        place = (row >> 5) * 24 + (row & 31)
        which = place >> 5
        hidden = place & 31
        return 16 * hidden + jnp.where(which == 2, 8, 0) + jnp.where(which == 1, 0, 1)

    order = one_hot_rows((E, 512), vector_source)
    vectors = jnp.dot(order, got_ref[:, 256:384], preferred_element_type=F32)
    in_quarter = lax.broadcasted_iota(jnp.int32, (32, E), 0)
    for k in range(4):
        base = QUARTER * k
        late_ref[base : base + 128, :] = local_v[128 * k : 128 * k + 128]
        small = vectors[32 * k : 32 * k + 32]
        small = jnp.where(in_quarter == 24, bias_ref[k : k + 1, :], small).astype(BF)
        for side in range(2):
            cols = slice(side * E, (side + 1) * E)
            at = 128 * k + 64 * side
            late_ref[base + 128 : base + 192, cols] = blocks[at : at + 64]
            late_ref[base + 192 : base + 208, cols] = small[16 * side : 16 * side + 16]
            at = base + 208 + 64 * side
            late_ref[at : at + 64, :] = up_ref[64 * k : 64 * k + 64, 256 * side : 256 * side + 256]
            at = 64 * k + 32 * side
            late_ref[base + 336 : base + 368, cols] = two_ref[at : at + 32, :]


def add_kernel(got_ref, out_ref):
    total = got_ref[:QUARTER, :].astype(F32)
    for k in range(1, 4):
        total = total + got_ref[QUARTER * k : QUARTER * (k + 1), :].astype(F32)
    for k in range(4):
        out_ref[QUARTER * k : QUARTER * (k + 1), :] = total.astype(BF)


def last_kernel(got_ref, v_ref, one_ref, small_ref, up_ref, two_ref):
    for k in range(4):
        base = QUARTER * k
        v_ref[128 * k : 128 * k + 128, :] = got_ref[base : base + 128, :].astype(F32)
        for side in range(2):
            cols = slice(side * E, (side + 1) * E)
            at = 128 * k + 64 * side
            one_ref[at : at + 64, :] = got_ref[base + 128 : base + 192, cols].astype(F32)
            at = 32 * k + 16 * side
            small_ref[at : at + 16, :] = got_ref[base + 192 : base + 208, cols].astype(F32)
            at = base + 208 + 64 * side
            up_ref[64 * k : 64 * k + 64, 256 * side : 256 * side + 256] = got_ref[
                at : at + 64, :
            ].astype(F32)
            at = 64 * k + 32 * side
            two_ref[at : at + 32, :] = got_ref[base + 336 : base + 368, cols].astype(F32)


def body(
    pooled,
    table_slot,
    cross_v,
    cross_u,
    cross_bias,
    block_index1,
    weight1,
    block_index2,
    weight2,
    top_vectors,
    labels,
    importance,
):
    tables = table_slot.shape[0]
    contract_last = (((1,), (1,)), ((), ()))
    core = lax.axis_index("table") % 2
    half_index = lax.dynamic_index_in_dim(block_index2.reshape(HB, 2, 2), core, 1, keepdims=False)
    half_index = half_index.reshape(-1)

    reads = block_index1[:, None] == table_slot[None, :]
    numbers = jnp.arange(tables, dtype=jnp.int32)
    block_of_slot = jnp.sum(jnp.where(reads, numbers[:, None], 0), axis=0)
    slot_of_block = jnp.sum(jnp.where(reads, numbers[None, :], 0), axis=1)
    block_of_slot = jnp.repeat(block_of_slot, 2)[:, None]
    slot_of_block = jnp.repeat(slot_of_block, 2)[:, None]
    hidden_of_slot = jnp.sum(
        jnp.where(reads, jnp.arange(tables, dtype=jnp.int32)[:, None] // K1, 0), axis=0
    )
    out_row = lax.broadcasted_iota(jnp.int32, (4, HB * 8, NT * 8), 1)
    in_row = lax.broadcasted_iota(jnp.int32, (4, HB * 8, NT * 8), 2)
    wanted = jnp.repeat(hidden_of_slot.reshape(NT, 4).T, 8, axis=1)[:, None, :]
    adds = ((wanted == out_row // 8) & (out_row % 8 == in_row % 8)).astype(BF)

    (sent,) = call(
        start_kernel,
        [jax.ShapeDtypeStruct((512, 384), BF)],
        pooled,
        cross_v,
        weight1.reshape(512, E),
    )
    got = exchange(sent.reshape(NT, 8, 384))
    half_two = lax.all_to_all(
        jnp.broadcast_to(weight2[None], (HB, 2, E, E)),
        "table",
        split_axis=0,
        concat_axis=0,
        tiled=True,
        axis_index_groups=[list(range(at, NT, 2)) for at in range(2)],
    ).reshape(NT, E, E)
    sent = regroup(got.reshape(512, 384), block_of_slot)
    arrived = exchange(sent.reshape(NT, 8, 384)).reshape(512, 384)
    lifted, factor, terms, weight_slot = lift(
        arrived, pooled, cross_u, cross_bias.reshape(1, 512)
    )
    got = exchange(terms.reshape(NT, 8, 512))
    preact_one, hidden_one = hidden_first(
        got.reshape(512, 512), adds, top_vectors[0].reshape(HB, E)
    )
    preact_one = preact_one.reshape(HB, 8, E).transpose(1, 0, 2)
    hidden_one = hidden_one.reshape(HB, 8, E).transpose(1, 0, 2)
    hidden_both = jnp.concatenate([hidden_one, from_sibling(hidden_one)], axis=0)
    picked_both = hidden_both[:, half_index]
    terms_two = jnp.einsum("bnc,ncd->bnd", picked_both, half_two, preferred_element_type=F32)
    half_sum = terms_two.reshape(16, HB, 2, E).sum(axis=2)
    preact_two = half_sum[:8] + from_sibling(half_sum[8:]) + top_vectors[1].reshape(-1, E)
    hidden_two = jax.nn.silu(preact_two).astype(BF)
    last_weight = top_vectors[2].reshape(-1, E)
    logit = jnp.sum(hidden_two.astype(F32) * last_weight, axis=(1, 2))
    sample_weight = importance.reshape(-1).astype(F32) / 8.0
    targets = labels.reshape(-1).astype(F32)
    grad_logit = sample_weight * (jax.nn.sigmoid(logit) - targets)
    grad_two = (grad_logit[:, None, None] * last_weight * silu_slope(preact_two)).astype(BF)
    last_terms = (hidden_two.astype(F32) * grad_logit[:, None, None]).astype(BF)
    grad_both = jnp.concatenate([grad_two, from_sibling(grad_two)], axis=0)
    spread_two = jnp.repeat(grad_both, 2, axis=1)
    back_two = jnp.einsum("bnd,ncd->bnc", spread_two, half_two, preferred_element_type=F32)
    onehot_two = (half_index[:, None] == jnp.arange(HB, dtype=jnp.int32)[None, :]).astype(F32)
    half_into = jnp.einsum("bnc,nj->bjc", back_two, onehot_two, precision=lax.Precision.HIGHEST)
    into_one = half_into[:8] + from_sibling(half_into[8:])
    grad_one = (into_one * silu_slope(preact_one)).astype(BF)

    spread_one = grad_one[:, hidden_of_slot].reshape(8, NT, 4 * E)
    picked_pair = hidden_one[:, block_index2].reshape(8, NT, 2 * E)
    both = jnp.repeat(grad_two, 2, axis=1)
    third = jnp.stack([grad_one, last_terms], axis=2).reshape(8, NT, E)
    sent = jnp.concatenate([spread_one, picked_pair, both, third], axis=2).transpose(1, 0, 2)
    got = exchange(sent).reshape(512, 8 * E)
    sent, direct, local_u, local_two, vector_rows, local_bias = call(
        owner_kernel,
        [
            jax.ShapeDtypeStruct((512, 384), BF),
            jax.ShapeDtypeStruct((512, 512), F32),
            jax.ShapeDtypeStruct((256, 512), BF),
            jax.ShapeDtypeStruct((256, E), BF),
            jax.ShapeDtypeStruct((8, E), F32),
            jax.ShapeDtypeStruct((8, E), F32),
        ],
        got,
        weight_slot,
        lifted,
        pooled,
        factor,
        arrived,
        cross_u,
    )
    got = exchange(sent.reshape(NT, 8, 384))
    sent = regroup(got.reshape(512, 384), slot_of_block, vector_rows)
    got = exchange(sent.reshape(NT, 8, 512)).reshape(512, 512)
    grad_crossed = got[:, :256]
    parts = [jax.ShapeDtypeStruct((4 * QUARTER, 256), BF)]
    (late,) = call(late_kernel, parts, got, pooled, local_u, local_two, local_bias)
    late = lax.all_to_all(late, "rep", split_axis=0, concat_axis=0, tiled=True)
    (late,) = call(add_kernel, parts, late)
    late = lax.all_to_all(late, "rep", split_axis=0, concat_axis=0, tiled=True)
    shapes = [(512, 256), (512, E), (E, E), (256, 512), (256, E)]
    grad_v, grad_w1, small, grad_u, grad_w2 = call(
        last_kernel, [jax.ShapeDtypeStruct(shape, F32) for shape in shapes], late
    )
    d_pooled = (
        direct + lax.dot_general(grad_crossed, cross_v, contract_last, preferred_element_type=F32)
    ).astype(BF)

    grad_w1 = grad_w1.reshape(4, E, E)
    grad_w2 = grad_w2.reshape(2, E, E)
    small = small.reshape(4, 32, E)
    grad_bias = small[:, 24].reshape(512)
    grad_vectors = small[:, :24].reshape(3, HB * E)
    return (d_pooled, grad_v, grad_u, grad_bias, grad_w1, grad_w2, grad_vectors)


def solution(mesh):
    placed = (
        P("rep", "table"),
        P(),
        P("table", None),
        P(None, "table"),
        P("table"),
        P(),
        P("table", None, None),
        P(),
        P("table", None, None),
        P(),
        P("rep", "table"),
        P("rep", "table"),
    )
    return jax.shard_map(
        body,
        mesh=mesh,
        in_specs=placed,
        out_specs=(
            P("rep", "table"),
            P("table", None),
            P(None, "table"),
            P("table"),
            P("table", None, None),
            P("table", None, None),
            P(),
        ),
        check_vma=False,
    )
```
